256 devices in a mesh: node: 16 (over y, x), local: 16 (over z, core).
Axes of the slice: x: 4, y: 4, z: 8, core: 2. Of those that a mesh axis runs over, the one named last changes fastest.
Arguments:
- inputs: bfloat16 [16384, 3584], P(('node', 'local')), may hold values from -6 to 6
- out_grad: bfloat16 [16384, 3584], P(('node', 'local')), may hold values from -6 to 6
- experts: int32 [16384, 2], P(('node', 'local')), may hold values from 0 to 127, as said below
- gate_values: bfloat16 [16384, 2], P(('node', 'local')), may hold values from 0.049804688 to 0.59765625
- gate_matrix: bfloat16 [256, 3584, 512], P(('node', 'local')), may hold values from -0.09375 to 0.09375
- up_matrix: bfloat16 [256, 3584, 512], P(('node', 'local')), may hold values from -0.09375 to 0.09375
- down_matrix: bfloat16 [256, 512, 3584], P(('node', 'local')), may hold values from -0.1875 to 0.1875
Outputs:
- input_grad: bfloat16 [16384, 3584], P(('node', 'local'))
The draws below stay inside these ranges and needn't reach their ends.
Inputs may be any that keep to these rules, and one draw needn't show every extreme that they name: Each token names 2 different experts, and both lie on the same node. Of the tokens of one device, at most 8 use one node and at most 2 name one expert; in every draw one node is used by exactly 8 tokens of every device, and each of its experts is named by exactly 2 tokens of every device.
All inputs are finite; a program needn't handle non-finite values.
Results may differ from the reference program's by a relative error of at most 0.0057.
Values may be sent and summed in bfloat16 or wider, within the bound.
A program may use at most 128 MiB of HBM per device.

```python
import math
import jax
import jax.numpy as jnp
from jax import lax

D = 3584
FF = 1024
TOPK = 2
NODES_TOK = 1
TOK_DEV = 64
HALF_FF = 512
EXPERTS = 128
TOKENS = 16384
HOST_ENTRY_CAP = 8
CAP = 2
N_NODE = 16
N_LOCAL = 16


def draw_experts(key, part):
    key = jax.random.fold_in(key, 7)
    blocks = N_NODE * N_LOCAL
    per_node = N_LOCAL // 2
    key_hot, key_order, key_score, key_perm = jax.random.split(key, 4)
    hot_node = jax.random.randint(key_hot, (), 0, N_NODE)
    orders = jax.vmap(lambda k: jax.random.permutation(k, TOK_DEV))(jax.random.split(key_order, blocks))
    placed = jnp.argsort(orders, axis=1)
    mandated_pick = placed < HOST_ENTRY_CAP
    node_range = jnp.arange(N_NODE, dtype=jnp.int32)
    dispatch_affinity = jax.random.randint(key_score, (blocks, TOK_DEV, N_NODE), 0, 1 << 20) * N_NODE + node_range
    crowded_marker = (node_range == hot_node).astype(jnp.int32)
    extra_affinity = 1 << 26
    dispatch_affinity = dispatch_affinity + jnp.where(mandated_pick[:, :, None], crowded_marker * extra_affinity, -crowded_marker * extra_affinity)

    def pick_nodes(block_scores):

        def step(sample_tallies, present_line):
            shifted_affinity = present_line - jnp.where(sample_tallies >= HOST_ENTRY_CAP, 4 * extra_affinity, 0)
            chosen = lax.top_k(shifted_affinity, NODES_TOK)[1]
            sample_tallies = sample_tallies + jnp.sum((chosen[:, None] == node_range).astype(jnp.int32), axis=0)
            return (sample_tallies, chosen)
        return lax.scan(step, jnp.zeros((N_NODE,), jnp.int32), block_scores)[1]
    picked = jax.vmap(pick_nodes)(dispatch_affinity).astype(jnp.int32)
    chosen_mask = jnp.any(picked[..., None] == node_range, axis=2).astype(jnp.int32)
    before = jnp.cumsum(chosen_mask, axis=1) - chosen_mask
    perm_keys = jax.random.split(key_perm, blocks * N_NODE * CAP)
    sequences = jax.vmap(lambda k: jax.random.permutation(k, per_node))(perm_keys).astype(jnp.int32)
    sequences = sequences.reshape(blocks, N_NODE, CAP * per_node)
    rank_pick = jnp.take_along_axis(before, picked, axis=2)
    picked_seq = sequences[jnp.arange(blocks)[:, None, None], picked]
    first = jnp.take_along_axis(picked_seq, (2 * rank_pick)[..., None], axis=3)[..., 0]
    second = jnp.take_along_axis(picked_seq, (2 * rank_pick + 1)[..., None], axis=3)[..., 0]
    ids = jnp.stack([picked * per_node + first, picked * per_node + second], axis=3)
    return ids.reshape(blocks * TOK_DEV, TOPK).astype(jnp.int32)


def shard_levels(stream_key, extent, cuts, smallest, high):
    level = 1.0
    for dim, shards_of in cuts:
        heights = jax.random.uniform(jax.random.fold_in(jax.random.fold_in(stream_key, 6), dim), (shards_of,), jnp.float32, smallest / len(cuts), high / len(cuts))
        level = level * jnp.repeat(jnp.exp(heights), extent[dim] // shards_of).reshape((-1,) + (1,) * (len(extent) - 1 - dim))
    return level


def noise(key, shape, scale, reach, cuts=(), kind=jnp.bfloat16):
    result = scale * jax.random.normal(key, shape, jnp.float32)
    if cuts:
        result = result * shard_levels(key, shape, cuts, -0.22, 0.18)
    return jnp.clip(result, -reach, reach).astype(kind)


def setup_inputs(seed: int = 0) -> dict:
    key_of = jax.random.split(jax.random.key(seed), 8)
    return {
        "inputs": noise(key_of[0], (TOKENS, D), 1.0, 6.0, ((0, 256),)),
        "out_grad": noise(key_of[1], (TOKENS, D), 1.0, 6.0, ((0, 256),)),
        "experts": draw_experts(jax.random.fold_in(key_of[7], 71), 0),
        "gate_values": jnp.clip(jnp.exp(math.log(0.59765625) - 2.4849066 * jax.random.uniform(key_of[3], (TOKENS, TOPK), jnp.float32) ** shard_levels(key_of[3], (TOKENS, TOPK), ((0, 256),), -0.2, 0.2)), 0.049804688, 0.59765625).astype(jnp.bfloat16),
        "gate_matrix": noise(key_of[4], (EXPERTS * 2, D, HALF_FF), D ** -0.5, 0.09375, ((0, 256),)),
        "up_matrix": noise(key_of[5], (EXPERTS * 2, D, HALF_FF), D ** -0.5, 0.09375, ((0, 256),)),
        "down_matrix": noise(key_of[6], (EXPERTS * 2, HALF_FF, D), FF ** -0.5, 0.1875, ((0, 256),)),
    }


def silu_backward(pre_gate, pre_up, hidden_grad):
    sig = jax.nn.sigmoid(pre_gate)
    grad_gate = hidden_grad * pre_up * sig * (1.0 + pre_gate * (1.0 - sig))
    grad_up = hidden_grad * pre_gate * sig
    return grad_gate.astype(jnp.bfloat16), grad_up.astype(jnp.bfloat16)


def reference(inputs, out_grad, experts, gate_values, gate_matrix, up_matrix, down_matrix):
    device_count = N_NODE * N_LOCAL
    per_node = N_LOCAL // 2
    expert_count = per_node * N_NODE
    tok_count = inputs.shape[0] // device_count
    ids = experts.reshape(device_count, tok_count, TOPK)
    expert_hits = ids[..., None] == jnp.arange(expert_count, dtype=jnp.int32)
    routed = jnp.any(expert_hits, axis=2).astype(jnp.int32)
    gate_table = jnp.sum(jnp.where(expert_hits, gate_values.reshape(device_count, tok_count, TOPK, 1).astype(jnp.float32), jnp.float32(0.0)), axis=2)
    slot_rank = jnp.cumsum(routed, axis=1) - routed
    slot_hit = (routed[..., None] == 1) & (slot_rank[..., None] == jnp.arange(CAP, dtype=jnp.int32))
    global_tok = jnp.arange(device_count * tok_count, dtype=jnp.int32).reshape(device_count, tok_count)
    token_of = jnp.sum(jnp.where(slot_hit, global_tok[:, :, None, None], 0), axis=1).astype(jnp.int32)
    gate_slot = jnp.sum(jnp.where(slot_hit, gate_table[..., None], jnp.float32(0.0)), axis=1)
    token_of = jnp.transpose(token_of, (1, 0, 2)).reshape(expert_count, device_count * CAP)
    gate_slot = jnp.transpose(gate_slot, (1, 0, 2)).reshape(expert_count, device_count * CAP)

    def add_half(expert_idx, half, accum):
        rows = token_of[expert_idx]
        gate_rows = gate_slot[expert_idx]
        x_rows = inputs[rows]
        grad_rows = out_grad[rows]
        index = 2 * expert_idx + half
        w_gate = gate_matrix[index]
        w_up = up_matrix[index]
        w_down = down_matrix[index]
        pre_gate = jnp.dot(x_rows, w_gate, preferred_element_type=jnp.float32)
        pre_up = jnp.dot(x_rows, w_up, preferred_element_type=jnp.float32)
        hidden_grad = gate_rows[:, None] * jnp.dot(grad_rows, w_down.T, preferred_element_type=jnp.float32)
        grad_gate, grad_up = silu_backward(pre_gate, pre_up, hidden_grad)
        part = jnp.dot(grad_gate, w_gate.T, preferred_element_type=jnp.float32) + jnp.dot(grad_up, w_up.T, preferred_element_type=jnp.float32)
        part = part.astype(jnp.bfloat16)
        return accum.at[rows].add(part.astype(jnp.float32))

    def node_step(node_idx, total):
        def expert_step(local_idx, accum):
            expert_idx = node_idx * per_node + local_idx
            accum = add_half(expert_idx, 0, accum)
            return add_half(expert_idx, 1, accum)

        accum = lax.fori_loop(0, per_node, expert_step, jnp.zeros(inputs.shape, jnp.float32))
        rounded = lax.optimization_barrier(accum.astype(jnp.bfloat16))
        return total + rounded.astype(jnp.float32)

    total = lax.fori_loop(0, N_NODE, node_step, jnp.zeros(inputs.shape, jnp.float32))
    return total.astype(jnp.bfloat16)
```

```python
import functools

import jax
import jax.numpy as jnp
from jax import lax
from jax.experimental import pallas as pl
from jax.experimental.pallas import tpu as pltpu
from jax.sharding import PartitionSpec as P

SLOTS = 2
CHUNK = 512
AHEAD = 2
MESH = pl.DeviceIdType.MESH
LAST = (((1,), (1,)), ((), ()))
F32 = jnp.float32
BF16 = jnp.bfloat16


def iota(shape, dim):
    return lax.broadcasted_iota(jnp.int32, shape, dim)


def kernel(
    nodes, zs, chunks, width,
    x_ref, g_ref, exp_ref, gate_ref, wg_hbm, wu_hbm, wd_hbm, out_ref,
    pick, combine, sort_in, sort_out, wg, wu, wd, acc_a, acc_b, acc_d, da, db,
    z_send, z_recv, n_send, n_recv, own, half_send, half_recv,
    back_send, back_recv, home_send, home_recv,
    w_sem, send_sem, recv_sem, local_sem,
):
    node = lax.axis_index("node")
    local = lax.axis_index("local")
    z = local // 2
    core = local % 2
    sibling = z * 2 + (1 - core)
    toks = x_ref.shape[0]
    per_z = nodes * SLOTS
    per_n = zs * SLOTS
    slots = nodes * zs * SLOTS

    weights = [
        pltpu.make_async_copy(src.at[0], dst, w_sem.at[i])
        for i, (src, dst) in enumerate(((wg_hbm, wg), (wu_hbm, wu), (wd_hbm, wd)))
    ]
    for copy in weights:
        copy.start()

    barrier = pltpu.get_barrier_semaphore()
    for j in range(1, zs):
        pl.semaphore_signal(
            barrier, inc=1, device_id=(node, lax.rem(z + j, zs) * 2 + core), device_id_type=MESH
        )
    for j in range(1, nodes):
        pl.semaphore_signal(
            barrier, inc=1, device_id=(lax.rem(node + j, nodes), local), device_id_type=MESH
        )
    pl.semaphore_signal(barrier, inc=1, device_id=(node, sibling), device_id_type=MESH)

    slot = iota((slots, toks), 0)
    expert = (slot % per_z) // SLOTS * zs + slot // per_z
    first = exp_ref[0:1, :] == expert
    second = exp_ref[1:2, :] == expert
    hit = (first | second).astype(F32)
    earlier = (iota((toks, toks), 0) < iota((toks, toks), 1)).astype(BF16)
    rank = jnp.dot(hit.astype(BF16), earlier, preferred_element_type=F32)
    chosen = jnp.where(rank == (slot % SLOTS).astype(F32), hit, 0.0)
    pick[...] = chosen.astype(BF16)
    gates = jnp.where(first, gate_ref[0:1, :].astype(F32), gate_ref[1:2, :].astype(F32))
    weighted = (chosen * gates).astype(BF16)
    eye = (iota((toks, toks), 0) == iota((toks, toks), 1)).astype(BF16)
    combine[...] = lax.dot_general(eye, weighted, LAST, preferred_element_type=F32).astype(BF16)
    row = iota((slots, slots), 0)
    col = iota((slots, slots), 1)
    wanted = (row % per_n) // SLOTS * per_z + row // per_n * SLOTS + row % SLOTS
    sort_in[...] = (col == wanted).astype(F32).astype(BF16)
    wanted = (row % per_z) // SLOTS * per_n + row // per_z * SLOTS + row % SLOTS
    sort_out[...] = (col == wanted).astype(F32).astype(BF16)
    acc_a[...] = jnp.zeros_like(acc_a)
    acc_b[...] = jnp.zeros_like(acc_b)
    acc_d[...] = jnp.zeros_like(acc_d)

    def columns(k):
        return pl.ds(pl.multiple_of(k * width, width), width)

    def remote(phase, k, src, dst, device):
        return pltpu.make_async_remote_copy(
            src_ref=src, dst_ref=dst, send_sem=send_sem.at[phase, k],
            recv_sem=recv_sem.at[phase, k], device_id=device, device_id_type=MESH,
        )

    def spread(phase, k, src, dst, along_z):
        here, count = (z, zs) if along_z else (node, nodes)
        pltpu.make_async_copy(src.at[here], dst.at[here], local_sem.at[phase, k]).start()
        for j in range(1, count):
            to = lax.rem(here + j, count)
            device = (node, to * 2 + core) if along_z else (to, local)
            remote(phase, k, src.at[to], dst.at[here], device).start()

    def arrive(phase, k, src, dst, along_z):
        here, count = (z, zs) if along_z else (node, nodes)
        pltpu.make_async_copy(src.at[here], dst.at[here], local_sem.at[phase, k]).wait()
        rest = pl.ds(0, count - 1)
        remote(phase, k, src.at[rest], dst.at[rest], (node, sibling)).wait_recv()

    def leave(phase, k, src, count):
        rest = pl.ds(0, count - 1)
        remote(phase, k, src.at[rest], src.at[rest], (node, sibling)).wait_send()

    def select(k):
        for part, ref in enumerate((x_ref, g_ref)):
            rows = jnp.dot(pick[...], ref[:, columns(k)], preferred_element_type=F32)
            z_send[k, :, part * per_z:(part + 1) * per_z, :] = rows.astype(BF16).reshape(
                zs, per_z, width
            )
        spread(0, k, z_send.at[k], z_recv.at[k], True)

    def resort(k):
        arrive(0, k, z_send.at[k], z_recv.at[k], True)
        for part in range(2):
            rows = z_recv[k, :, part * per_z:(part + 1) * per_z, :].reshape(slots, width)
            rows = jnp.dot(sort_in[...], rows, preferred_element_type=F32)
            n_send[k, :, part * per_n:(part + 1) * per_n, :] = rows.astype(BF16).reshape(
                nodes, per_n, width
            )
        spread(1, k, n_send.at[k], n_recv.at[k, 0], False)

    def share(k):
        arrive(1, k, n_send.at[k], n_recv.at[k, 0], False)
        remote(2, k, n_recv.at[k, 0], n_recv.at[k, 1], (node, sibling)).start()

    def multiply(k):
        remote(2, k, n_recv.at[k, 0], n_recv.at[k, 1], (node, sibling)).wait_recv()
        rows = n_recv[k, :, :, 0:per_n, :].reshape(2 * slots, width)
        acc_a[...] += jnp.dot(rows, wg[columns(k), :], preferred_element_type=F32)
        acc_b[...] += jnp.dot(rows, wu[columns(k), :], preferred_element_type=F32)
        rows = n_recv[k, :, :, per_n:2 * per_n, :].reshape(2 * slots, width)
        acc_d[...] += lax.dot_general(rows, wd[:, columns(k)], LAST, preferred_element_type=F32)

    def project(k):
        part = lax.dot_general(da[...], wg[columns(k), :], LAST, preferred_element_type=F32)
        part += lax.dot_general(db[...], wu[columns(k), :], LAST, preferred_element_type=F32)
        own[k] = part[0:slots]
        half_send[k] = part[slots:2 * slots].astype(BF16)
        remote(3, k, half_send.at[k], half_recv.at[k], (node, sibling)).start()

    def add_halves(k):
        remote(3, k, half_send.at[k], half_recv.at[k], (node, sibling)).wait_recv()
        rows = (own[k] + half_recv[k].astype(F32)).astype(BF16)
        back_send[k] = rows.reshape(nodes, per_n, width)
        spread(4, k, back_send.at[k], back_recv.at[k], False)

    def unsort(k):
        arrive(4, k, back_send.at[k], back_recv.at[k], False)
        rows = back_recv[k].reshape(slots, width)
        rows = jnp.dot(sort_out[...], rows, preferred_element_type=F32)
        home_send[k] = rows.astype(BF16).reshape(zs, per_z, width)
        spread(5, k, home_send.at[k], home_recv.at[k], True)

    def gather(k):
        arrive(5, k, home_send.at[k], home_recv.at[k], True)
        rows = home_recv[k].reshape(slots, width)
        out_ref[:, columns(k)] = jnp.dot(
            combine[...], rows, preferred_element_type=F32
        ).astype(BF16)

    def when(i, lag, stage):
        @pl.when((i >= lag) & (i < chunks + lag))
        def _():
            stage(i - lag)

    pl.semaphore_wait(barrier, zs + nodes - 1)

    def dispatch(i, carry):
        when(i, 0, select)
        when(i, AHEAD, resort)
        when(i, AHEAD + 1, share)

        @pl.when(i == AHEAD + 2)
        def _():
            for copy in weights:
                copy.wait()

        when(i, AHEAD + 2, multiply)
        return carry

    lax.fori_loop(0, chunks + AHEAD + 2, dispatch, 0)

    a = acc_a[...]
    sig = jax.nn.sigmoid(a)
    grad = acc_d[...] * sig
    da[...] = (grad * acc_b[...] * (1.0 + a * (1.0 - sig))).astype(BF16)
    db[...] = (grad * a).astype(BF16)

    def combine_step(i, carry):
        when(i, 0, project)
        when(i, 1, add_halves)
        when(i, 2, unsort)
        when(i, 4, gather)
        return carry

    lax.fori_loop(0, chunks + 4, combine_step, 0)

    def drain(k, carry):
        leave(0, k, z_send.at[k], zs)
        leave(1, k, n_send.at[k], nodes)
        remote(2, k, n_recv.at[k, 0], n_recv.at[k, 1], (node, sibling)).wait_send()
        remote(3, k, half_send.at[k], half_recv.at[k], (node, sibling)).wait_send()
        leave(4, k, back_send.at[k], nodes)
        leave(5, k, home_send.at[k], zs)
        return carry

    lax.fori_loop(0, chunks, drain, 0)


def shards(inputs, out_grad, experts, gate_values, gate_matrix, up_matrix, down_matrix):
    nodes = lax.axis_size("node")
    zs = lax.axis_size("local") // 2
    toks, model = inputs.shape
    hidden = gate_matrix.shape[2]
    width = CHUNK
    chunks = model // width
    per_z = nodes * SLOTS
    per_n = zs * SLOTS
    slots = nodes * zs * SLOTS
    vmem = pl.BlockSpec(memory_space=pltpu.VMEM)
    hbm = pl.BlockSpec(memory_space=pl.ANY)
    return pl.pallas_call(
        functools.partial(kernel, nodes, zs, chunks, width),
        out_shape=jax.ShapeDtypeStruct((toks, model), BF16),
        in_specs=[vmem] * 4 + [hbm] * 3,
        out_specs=vmem,
        scratch_shapes=[
            pltpu.VMEM((slots, toks), BF16),
            pltpu.VMEM((toks, slots), BF16),
            pltpu.VMEM((slots, slots), BF16),
            pltpu.VMEM((slots, slots), BF16),
            pltpu.VMEM((model, hidden), BF16),
            pltpu.VMEM((model, hidden), BF16),
            pltpu.VMEM((hidden, model), BF16),
            pltpu.VMEM((2 * slots, hidden), F32),
            pltpu.VMEM((2 * slots, hidden), F32),
            pltpu.VMEM((2 * slots, hidden), F32),
            pltpu.VMEM((2 * slots, hidden), BF16),
            pltpu.VMEM((2 * slots, hidden), BF16),
            pltpu.VMEM((chunks, zs, 2 * per_z, width), BF16),
            pltpu.VMEM((chunks, zs, 2 * per_z, width), BF16),
            pltpu.VMEM((chunks, nodes, 2 * per_n, width), BF16),
            pltpu.VMEM((chunks, 2, nodes, 2 * per_n, width), BF16),
            pltpu.VMEM((chunks, slots, width), F32),
            pltpu.VMEM((chunks, slots, width), BF16),
            pltpu.VMEM((chunks, slots, width), BF16),
            pltpu.VMEM((chunks, nodes, per_n, width), BF16),
            pltpu.VMEM((chunks, nodes, per_n, width), BF16),
            pltpu.VMEM((chunks, zs, per_z, width), BF16),
            pltpu.VMEM((chunks, zs, per_z, width), BF16),
            pltpu.SemaphoreType.DMA((3,)),
            pltpu.SemaphoreType.DMA((6, chunks)),
            pltpu.SemaphoreType.DMA((6, chunks)),
            pltpu.SemaphoreType.DMA((6, chunks)),
        ],
        compiler_params=pltpu.CompilerParams(
            collective_id=0, has_side_effects=True, vmem_limit_bytes=60 * 1024 * 1024
        ),
        name="experts_backward",
    )(
        inputs, out_grad, experts.T, gate_values.T, gate_matrix, up_matrix, down_matrix
    )


def solution(mesh):
    rows = P(("node", "local"), None)
    stack = P(("node", "local"), None, None)
    return jax.shard_map(
        shards, mesh=mesh, in_specs=(rows,) * 4 + (stack,) * 3, out_specs=rows, check_vma=False
    )
```

```python
import functools

import jax
import jax.numpy as jnp
from jax import lax
from jax.experimental import pallas as pl
from jax.experimental.pallas import tpu as pltpu
from jax.sharding import PartitionSpec as P

SLOTS = 2
CAP = 24
CHUNK = 512
BACK_CHUNK = 512
AHEAD = 2
MESH = pl.DeviceIdType.MESH
LAST = (((1,), (1,)), ((), ()))
F32 = jnp.float32
BF16 = jnp.bfloat16


def iota(shape, dim):
    return lax.broadcasted_iota(jnp.int32, shape, dim)


def eye(n):
    return (iota((n, n), 0) == iota((n, n), 1)).astype(BF16)


def kernel(
    nodes, zs, cap, chunks, width, back_chunks, back_width,
    x_ref, g_ref, exp_ref, gate_ref, wg_hbm, wu_hbm, wd_hbm, out_ref, flag_ref,
    pick_x, pick_g, comb_lo, comb_hi, sort_x, sort_g, list_lo, list_hi,
    wg, wu, wd, acc_a, acc_b, acc_d, da, db,
    z_send, z_recv, n_send, n_recv, own, half_send, half_recv,
    back_send, back_recv, home_send, home_recv,
    meta_send, meta_recv, flag_n_send, flag_n_recv, flag_s_send, flag_s_recv,
    w_sem, send_sem, recv_sem, local_sem,
):
    node = lax.axis_index("node")
    local = lax.axis_index("local")
    z = local // 2
    core = local % 2
    sibling = (node, z * 2 + (1 - core))
    toks = x_ref.shape[0]
    per_n = zs * SLOTS
    slots = nodes * zs * SLOTS
    block = 2 * cap
    listed = zs * block

    weights = [
        pltpu.make_async_copy(src.at[0], dst, w_sem.at[i])
        for i, (src, dst) in enumerate(((wg_hbm, wg), (wu_hbm, wu), (wd_hbm, wd)))
    ]
    for copy in weights:
        copy.start()

    barrier = pltpu.get_barrier_semaphore()
    for j in range(1, zs):
        pl.semaphore_signal(
            barrier, inc=1, device_id=(node, lax.rem(z + j, zs) * 2 + core), device_id_type=MESH
        )
    for j in range(1, nodes):
        pl.semaphore_signal(
            barrier, inc=1, device_id=(lax.rem(node + j, nodes), local), device_id_type=MESH
        )
    pl.semaphore_signal(barrier, inc=1, device_id=sibling, device_id_type=MESH)

    earlier = (iota((toks, toks), 0) < iota((toks, toks), 1)).astype(BF16)

    def before(mask):
        return jnp.dot(mask.astype(BF16), earlier, preferred_element_type=F32)

    first = exp_ref[0:1, :]
    second = exp_ref[1:2, :]
    target = iota((listed, toks), 0) // block
    half = (iota((listed, toks), 0) % block) // cap
    place = (iota((listed, toks), 0) % cap).astype(F32)
    by_first = lax.rem(first, zs) == target
    by_second = lax.rem(second, zs) == target
    on_list = (by_first | by_second).astype(F32)
    chosen = jnp.where(before(on_list) == place, on_list, 0.0)
    pick_x[...] = jnp.where(half == 0, chosen, 0.0).astype(BF16)
    pick_g[...] = jnp.where(half == 1, chosen, 0.0).astype(BF16)
    gates = jnp.where(by_first, gate_ref[0:1, :].astype(F32), gate_ref[1:2, :].astype(F32))
    weighted = chosen * gates
    turn = eye(toks)
    for h, ref in enumerate((comb_lo, comb_hi)):
        ref[...] = lax.dot_general(
            turn, jnp.where(half == h, weighted, 0.0).astype(BF16), LAST,
            preferred_element_type=F32,
        ).astype(BF16)
    longest = jnp.max(jnp.sum(on_list, axis=1, keepdims=True), axis=0, keepdims=True)
    over = (longest > cap).astype(F32).astype(jnp.int32)
    meta_send[...] = jnp.zeros_like(meta_send) + over
    meta_send[0:1, 0:toks] = first
    meta_send[1:2, 0:toks] = second
    acc_a[...] = jnp.zeros_like(acc_a)
    acc_b[...] = jnp.zeros_like(acc_b)
    acc_d[...] = jnp.zeros_like(acc_d)

    def columns(k, size):
        return pl.ds(pl.multiple_of(k * size, size), size)

    def remote(phase, k, src, dst, device):
        return pltpu.make_async_remote_copy(
            src_ref=src, dst_ref=dst, send_sem=send_sem.at[phase, k],
            recv_sem=recv_sem.at[phase, k], device_id=device, device_id_type=MESH,
        )

    def spread(phase, k, src, dst, along_z, shared=False):
        here, count = (z, zs) if along_z else (node, nodes)
        mine = src if shared else src.at[here]
        pltpu.make_async_copy(mine, dst.at[here], local_sem.at[phase, k]).start()
        for j in range(1, count):
            to = lax.rem(here + j, count)
            device = (node, to * 2 + core) if along_z else (to, local)
            remote(phase, k, src if shared else src.at[to], dst.at[here], device).start()

    def arrive(phase, k, dst, along_z):
        here, count = (z, zs) if along_z else (node, nodes)
        pltpu.make_async_copy(dst.at[here], dst.at[here], local_sem.at[phase, k]).wait()
        rest = pl.ds(0, count - 1)
        remote(phase, k, dst.at[rest], dst.at[rest], sibling).wait_recv()

    def leave(phase, k, dst, count):
        rest = pl.ds(0, count - 1)
        remote(phase, k, dst.at[rest], dst.at[rest], sibling).wait_send()

    def select(k):
        rows = jnp.dot(pick_x[...], x_ref[:, columns(k, width)], preferred_element_type=F32)
        rows += jnp.dot(pick_g[...], g_ref[:, columns(k, width)], preferred_element_type=F32)
        z_send[k] = rows.astype(BF16).reshape(zs, block, width)
        spread(0, k, z_send.at[k], z_recv.at[k], True)

    def resort(k):
        arrive(0, k, z_recv.at[k], True)
        rows = z_recv[k].reshape(listed, width)
        for h, ref in enumerate((sort_x, sort_g)):
            part = jnp.dot(ref[...], rows, preferred_element_type=F32)
            n_send[k, :, h * per_n:(h + 1) * per_n, :] = part.astype(BF16).reshape(
                nodes, per_n, width
            )
        spread(1, k, n_send.at[k], n_recv.at[k, 0], False)

    def share(k):
        arrive(1, k, n_recv.at[k, 0], False)
        remote(2, k, n_recv.at[k, 0], n_recv.at[k, 1], sibling).start()

    def multiply(k):
        remote(2, k, n_recv.at[k, 0], n_recv.at[k, 1], sibling).wait_recv()
        rows = n_recv[k, :, :, 0:per_n, :].reshape(2 * slots, width)
        acc_a[...] += jnp.dot(rows, wg[columns(k, width), :], preferred_element_type=F32)
        acc_b[...] += jnp.dot(rows, wu[columns(k, width), :], preferred_element_type=F32)
        rows = n_recv[k, :, :, per_n:2 * per_n, :].reshape(2 * slots, width)
        acc_d[...] += lax.dot_general(
            rows, wd[:, columns(k, width)], LAST, preferred_element_type=F32
        )

    def project(k):
        cols = columns(k, back_width)
        part = lax.dot_general(da[...], wg[cols, :], LAST, preferred_element_type=F32)
        part += lax.dot_general(db[...], wu[cols, :], LAST, preferred_element_type=F32)
        own[k] = part[0:slots]
        half_send[k] = part[slots:2 * slots].astype(BF16)
        remote(3, k, half_send.at[k], half_recv.at[k], sibling).start()

    def add_halves(k):
        remote(3, k, half_send.at[k], half_recv.at[k], sibling).wait_recv()
        rows = (own[k] + half_recv[k].astype(F32)).astype(BF16)
        back_send[k] = rows.reshape(nodes, per_n, back_width)
        spread(4, k, back_send.at[k], back_recv.at[k], False)

    mid = back_width // 2

    def unsort(k):
        arrive(4, k, back_recv.at[k], False)
        rows = jnp.dot(
            list_lo[...], back_recv[k, :, :, 0:mid].reshape(slots, mid),
            preferred_element_type=F32,
        )
        rows += jnp.dot(
            list_hi[...], back_recv[k, :, :, mid:back_width].reshape(slots, mid),
            preferred_element_type=F32,
        )
        home_send[k] = rows.astype(BF16).reshape(zs, block, mid)
        spread(5, k, home_send.at[k], home_recv.at[k], True)

    def gather(k):
        arrive(5, k, home_recv.at[k], True)
        rows = home_recv[k].reshape(listed, mid)
        for h, ref in enumerate((comb_lo, comb_hi)):
            out_ref[:, pl.ds(pl.multiple_of(k * back_width + h * mid, mid), mid)] = jnp.dot(
                ref[...], rows, preferred_element_type=F32
            ).astype(BF16)

    def when(i, lag, count, stage):
        @pl.when((i >= lag) & (i < count + lag))
        def _():
            stage(i - lag)

    pl.semaphore_wait(barrier, zs + nodes - 1)
    spread(6, 0, meta_send, meta_recv, True, shared=True)
    for k in range(min(AHEAD, chunks)):
        select(k)

    arrive(6, 0, meta_recv, True)
    slot = iota((nodes * SLOTS, toks), 0)
    expert = slot // SLOTS * zs + z
    wanted = (slot % SLOTS).astype(F32)
    position = (iota((block, toks), 0) % cap).astype(F32)
    wide = iota((nodes * SLOTS, slots), 1)
    narrow = iota((nodes * SLOTS, slots), 0)
    same = (wide // per_n == narrow // SLOTS) & (wide % SLOTS == narrow % SLOTS)
    lower = iota((block, slots), 0) // cap
    flags = meta_recv[0]
    for q in range(zs):
        if q:
            flags = jnp.maximum(flags, meta_recv[q])
        first = meta_recv[q, 0:1, 0:toks]
        second = meta_recv[q, 1:2, 0:toks]
        names = ((first == expert) | (second == expert)).astype(F32)
        names = jnp.where(before(names) == wanted, names, 0.0)
        on_list = (lax.rem(first, zs) == z) | (lax.rem(second, zs) == z)
        on_list = jnp.broadcast_to(on_list.astype(F32), (block, toks))
        on_list = jnp.where(before(on_list) == position, on_list, 0.0)
        table = lax.dot_general(
            on_list.astype(BF16), names.astype(BF16), LAST, preferred_element_type=F32
        )
        place_q = (same & ((wide % per_n) // SLOTS == q)).astype(F32).astype(BF16)
        table = jnp.dot(table.astype(BF16), place_q, preferred_element_type=F32)
        list_lo[q * block:(q + 1) * block, :] = jnp.where(lower == 0, table, 0.0).astype(BF16)
        list_hi[q * block:(q + 1) * block, :] = jnp.where(lower == 1, table, 0.0).astype(BF16)
    turn = eye(slots)
    sort_x[...] = lax.dot_general(turn, list_lo[...], LAST, preferred_element_type=F32).astype(BF16)
    sort_g[...] = lax.dot_general(turn, list_hi[...], LAST, preferred_element_type=F32).astype(BF16)
    flag_n_send[...] = flags
    spread(7, 0, flag_n_send, flag_n_recv, False, shared=True)

    def dispatch(i, carry):
        @pl.when(i + AHEAD < chunks)
        def _():
            select(i + AHEAD)

        when(i, 0, chunks, resort)
        when(i, 1, chunks, share)

        @pl.when(i == 2)
        def _():
            for copy in weights:
                copy.wait()

        when(i, 2, chunks, multiply)
        return carry

    lax.fori_loop(0, chunks + 2, dispatch, 0)

    a = acc_a[...]
    sig = jax.nn.sigmoid(a)
    grad = acc_d[...] * sig
    da[...] = (grad * acc_b[...] * (1.0 + a * (1.0 - sig))).astype(BF16)
    db[...] = (grad * a).astype(BF16)

    def combine_step(i, carry):
        when(i, 0, back_chunks, project)
        when(i, 1, back_chunks, add_halves)
        when(i, 2, back_chunks, unsort)
        when(i, 4, back_chunks, gather)
        return carry

    lax.fori_loop(0, back_chunks + 4, combine_step, 0)

    arrive(7, 0, flag_n_recv, False)
    flags = flag_n_recv[0]
    for m in range(1, nodes):
        flags = jnp.maximum(flags, flag_n_recv[m])
    flag_s_send[...] = flags
    other = remote(8, 0, flag_s_send, flag_s_recv, sibling)
    other.start()
    other.wait_recv()
    flag_ref[...] = jnp.maximum(flags, flag_s_recv[...])

    def drain(k, carry):
        leave(0, k, z_recv.at[k], zs)
        leave(1, k, n_recv.at[k, 0], nodes)
        remote(2, k, n_recv.at[k, 0], n_recv.at[k, 1], sibling).wait_send()
        return carry

    lax.fori_loop(0, chunks, drain, 0)

    def drain_back(k, carry):
        remote(3, k, half_send.at[k], half_recv.at[k], sibling).wait_send()
        leave(4, k, back_recv.at[k], nodes)
        leave(5, k, home_recv.at[k], zs)
        return carry

    lax.fori_loop(0, back_chunks, drain_back, 0)
    leave(6, 0, meta_recv, zs)
    leave(7, 0, flag_n_recv, nodes)
    other.wait_send()


def exchange(cap, collective, inputs, out_grad, experts, gates, gate_matrix, up_matrix, down_matrix):
    nodes = lax.axis_size("node")
    zs = lax.axis_size("local") // 2
    toks, model = inputs.shape
    hidden = gate_matrix.shape[2]
    width, back_width = CHUNK, BACK_CHUNK
    chunks, back_chunks = model // width, model // back_width
    per_n = zs * SLOTS
    slots = nodes * zs * SLOTS
    block = 2 * cap
    listed = zs * block
    steps = max(chunks, back_chunks)
    vmem = pl.BlockSpec(memory_space=pltpu.VMEM)
    hbm = pl.BlockSpec(memory_space=pl.ANY)
    return pl.pallas_call(
        functools.partial(kernel, nodes, zs, cap, chunks, width, back_chunks, back_width),
        out_shape=(
            jax.ShapeDtypeStruct((toks, model), BF16),
            jax.ShapeDtypeStruct((8, 128), jnp.int32),
        ),
        in_specs=[vmem] * 4 + [hbm] * 3,
        out_specs=(vmem, vmem),
        scratch_shapes=[
            pltpu.VMEM((listed, toks), BF16),
            pltpu.VMEM((listed, toks), BF16),
            pltpu.VMEM((toks, listed), BF16),
            pltpu.VMEM((toks, listed), BF16),
            pltpu.VMEM((slots, listed), BF16),
            pltpu.VMEM((slots, listed), BF16),
            pltpu.VMEM((listed, slots), BF16),
            pltpu.VMEM((listed, slots), BF16),
            pltpu.VMEM((model, hidden), BF16),
            pltpu.VMEM((model, hidden), BF16),
            pltpu.VMEM((hidden, model), BF16),
            pltpu.VMEM((2 * slots, hidden), F32),
            pltpu.VMEM((2 * slots, hidden), F32),
            pltpu.VMEM((2 * slots, hidden), F32),
            pltpu.VMEM((2 * slots, hidden), BF16),
            pltpu.VMEM((2 * slots, hidden), BF16),
            pltpu.VMEM((chunks, zs, block, width), BF16),
            pltpu.VMEM((chunks, zs, block, width), BF16),
            pltpu.VMEM((chunks, nodes, 2 * per_n, width), BF16),
            pltpu.VMEM((chunks, 2, nodes, 2 * per_n, width), BF16),
            pltpu.VMEM((back_chunks, slots, back_width), F32),
            pltpu.VMEM((back_chunks, slots, back_width), BF16),
            pltpu.VMEM((back_chunks, slots, back_width), BF16),
            pltpu.VMEM((back_chunks, nodes, per_n, back_width), BF16),
            pltpu.VMEM((back_chunks, nodes, per_n, back_width), BF16),
            pltpu.VMEM((back_chunks, zs, block, back_width // 2), BF16),
            pltpu.VMEM((back_chunks, zs, block, back_width // 2), BF16),
            pltpu.VMEM((8, 128), jnp.int32),
            pltpu.VMEM((zs, 8, 128), jnp.int32),
            pltpu.VMEM((8, 128), jnp.int32),
            pltpu.VMEM((nodes, 8, 128), jnp.int32),
            pltpu.VMEM((8, 128), jnp.int32),
            pltpu.VMEM((8, 128), jnp.int32),
            pltpu.SemaphoreType.DMA((3,)),
            pltpu.SemaphoreType.DMA((9, steps)),
            pltpu.SemaphoreType.DMA((9, steps)),
            pltpu.SemaphoreType.DMA((9, steps)),
        ],
        compiler_params=pltpu.CompilerParams(
            collective_id=collective, has_side_effects=True, vmem_limit_bytes=60 * 1024 * 1024
        ),
        name=f"experts_backward_{cap}",
    )(inputs, out_grad, experts, gates, gate_matrix, up_matrix, down_matrix)


def shards(inputs, out_grad, experts, gate_values, gate_matrix, up_matrix, down_matrix):
    nodes = lax.axis_size("node")
    args = (inputs, out_grad, experts.T, gate_values.T, gate_matrix, up_matrix, down_matrix)
    result, flags = exchange(CAP, 0, *args)
    return lax.cond(
        flags[7, 127] > 0,
        lambda: exchange(nodes * SLOTS, 1, *args)[0],
        lambda: result,
    )


def solution(mesh):
    rows = P(("node", "local"), None)
    stack = P(("node", "local"), None, None)
    return jax.shard_map(
        shards, mesh=mesh, in_specs=(rows,) * 4 + (stack,) * 3, out_specs=rows, check_vma=False
    )
```

```python
import functools

import jax
import jax.numpy as jnp
from jax import lax
from jax.experimental import pallas as pl
from jax.experimental.pallas import tpu as pltpu
from jax.sharding import PartitionSpec as P

SLOTS = 2
CAP = 24
OUT_SEGMENTS = ((5, 512), (2, 256), (4, 128))
BACK_SEGMENTS = ((1, 256), (6, 512), (1, 256))
AHEAD = 2
MESH = pl.DeviceIdType.MESH
LAST = (((1,), (1,)), ((), ()))
F32 = jnp.float32
BF16 = jnp.bfloat16


def iota(shape, dim):
    return lax.broadcasted_iota(jnp.int32, shape, dim)


def eye(n):
    return (iota((n, n), 0) == iota((n, n), 1)).astype(BF16)


class Chunk:
    def __init__(self, segment, k):
        self.buffers, self.width, self.begin, self.first = segment
        self.k = k
        self.sem = self.first + k

    def columns(self, part=0, parts=1):
        size = self.width // parts
        start = self.begin + self.k * self.width + part * size
        return pl.ds(start if isinstance(start, int) else pl.multiple_of(start, 128), size)

    def at(self, i, *rest):
        return self.buffers[i].at[(self.k, *rest)]

    def get(self, i):
        return self.buffers[i][self.k]


def split(segments, refs):
    result, begin, first = [], 0, 0
    each = len(refs) // len(segments)
    for n, (count, width) in enumerate(segments):
        result.append(((refs[n * each:(n + 1) * each], width, begin, first), count))
        begin += count * width
        first += count
    return result, first


def kernel(
    nodes, zs, cap,
    x_ref, g_ref, exp_ref, gate_ref, wg_hbm, wu_hbm, wd_hbm, out_ref, flag_ref,
    pick_x, pick_g, comb_lo, comb_hi, sort_x, sort_g, list_lo, list_hi,
    wg, wu, wd, acc_a, acc_b, acc_d, da, db,
    meta_send, meta_recv, flag_n_send, flag_n_recv, flag_s_send, flag_s_recv,
    w_sem, send_sem, recv_sem, local_sem, *rest,
):
    z_send, z_recv, n_send, n_recv = range(4)
    own, half_send, half_recv, back_send, back_recv, home_send, home_recv = range(7)
    out_segments, out_steps = split(OUT_SEGMENTS, rest[:4 * len(OUT_SEGMENTS)])
    back_segments, back_steps = split(BACK_SEGMENTS, rest[4 * len(OUT_SEGMENTS):])
    node = lax.axis_index("node")
    local = lax.axis_index("local")
    z = local // 2
    core = local % 2
    sibling = (node, z * 2 + (1 - core))
    toks = x_ref.shape[0]
    per_n = zs * SLOTS
    slots = nodes * zs * SLOTS
    block = 2 * cap
    listed = zs * block

    weights = [
        pltpu.make_async_copy(src.at[0], dst, w_sem.at[i])
        for i, (src, dst) in enumerate(((wg_hbm, wg), (wu_hbm, wu), (wd_hbm, wd)))
    ]
    for copy in weights:
        copy.start()

    barrier = pltpu.get_barrier_semaphore()
    for j in range(1, zs):
        pl.semaphore_signal(
            barrier, inc=1, device_id=(node, lax.rem(z + j, zs) * 2 + core), device_id_type=MESH
        )
    for j in range(1, nodes):
        pl.semaphore_signal(
            barrier, inc=1, device_id=(lax.rem(node + j, nodes), local), device_id_type=MESH
        )
    pl.semaphore_signal(barrier, inc=1, device_id=sibling, device_id_type=MESH)

    earlier = (iota((toks, toks), 0) < iota((toks, toks), 1)).astype(BF16)

    def before(mask):
        return jnp.dot(mask.astype(BF16), earlier, preferred_element_type=F32)

    first = exp_ref[0:1, :]
    second = exp_ref[1:2, :]
    target = iota((zs, toks), 0)
    by_first = lax.rem(first, zs) == target
    by_second = lax.rem(second, zs) == target
    on_list = (by_first | by_second).astype(F32)

    def expand(rows):
        return jnp.broadcast_to(rows[:, None, :], (zs, block, toks)).reshape(listed, toks)

    order = iota((zs, block, toks), 1).reshape(listed, toks)
    upper = order >= cap
    place = jnp.where(upper, order - cap, order).astype(F32)
    chosen = jnp.where(expand(before(on_list)) == place, expand(on_list), 0.0)
    pick_x[...] = jnp.where(upper, 0.0, chosen).astype(BF16)
    pick_g[...] = jnp.where(upper, chosen, 0.0).astype(BF16)
    longest = jnp.max(jnp.sum(on_list, axis=1, keepdims=True), axis=0, keepdims=True)
    over = (longest > cap).astype(F32).astype(jnp.int32)
    meta_send[...] = jnp.zeros_like(meta_send) + over
    meta_send[0:1, 0:toks] = first
    meta_send[1:2, 0:toks] = second

    def remote(phase, k, src, dst, device):
        return pltpu.make_async_remote_copy(
            src_ref=src, dst_ref=dst, send_sem=send_sem.at[phase, k],
            recv_sem=recv_sem.at[phase, k], device_id=device, device_id_type=MESH,
        )

    def spread(phase, k, src, dst, along_z, shared=False):
        here, count = (z, zs) if along_z else (node, nodes)
        mine = src if shared else src.at[here]
        pltpu.make_async_copy(mine, dst.at[here], local_sem.at[phase, k]).start()
        for j in range(1, count):
            to = lax.rem(here + j, count)
            device = (node, to * 2 + core) if along_z else (to, local)
            remote(phase, k, src if shared else src.at[to], dst.at[here], device).start()

    def arrive(phase, k, dst, along_z):
        here, count = (z, zs) if along_z else (node, nodes)
        pltpu.make_async_copy(dst.at[here], dst.at[here], local_sem.at[phase, k]).wait()
        rest = pl.ds(0, count - 1)
        remote(phase, k, dst.at[rest], dst.at[rest], sibling).wait_recv()

    def leave(phase, k, dst, count):
        rest = pl.ds(0, count - 1)
        remote(phase, k, dst.at[rest], dst.at[rest], sibling).wait_send()

    def select(c):
        rows = jnp.dot(pick_x[...], x_ref[:, c.columns()], preferred_element_type=F32)
        rows += jnp.dot(pick_g[...], g_ref[:, c.columns()], preferred_element_type=F32)
        c.buffers[z_send][c.k] = rows.astype(BF16).reshape(zs, block, c.width)
        spread(0, c.sem, c.at(z_send), c.at(z_recv), True)

    def resort(c):
        arrive(0, c.sem, c.at(z_recv), True)
        rows = c.get(z_recv).reshape(listed, c.width)
        for h, ref in enumerate((sort_x, sort_g)):
            part = jnp.dot(ref[...], rows, preferred_element_type=F32)
            c.buffers[n_send][c.k, :, h * per_n:(h + 1) * per_n, :] = part.astype(BF16).reshape(
                nodes, per_n, c.width
            )
        spread(1, c.sem, c.at(n_send), c.at(n_recv, 0), False)

    def to_sibling(c):
        return remote(2, c.sem, c.at(n_recv, 0), c.at(n_recv, 1), sibling)

    def share(c):
        arrive(1, c.sem, c.at(n_recv, 0), False)
        to_sibling(c).start()

    def multiply(c):
        to_sibling(c).wait_recv()
        cols = c.columns()
        rows = c.buffers[n_recv][c.k, :, :, 0:per_n, :].reshape(2 * slots, c.width)
        acc_a[...] += jnp.dot(rows, wg[cols, :], preferred_element_type=F32)
        acc_b[...] += jnp.dot(rows, wu[cols, :], preferred_element_type=F32)
        rows = c.buffers[n_recv][c.k, :, :, per_n:2 * per_n, :].reshape(2 * slots, c.width)
        acc_d[...] += lax.dot_general(rows, wd[:, cols], LAST, preferred_element_type=F32)

    def release(c):
        leave(0, c.sem, c.at(z_recv), zs)
        leave(1, c.sem, c.at(n_recv, 0), nodes)
        to_sibling(c).wait_send()

    def halves(c):
        return remote(3, c.sem, c.at(half_send), c.at(half_recv), sibling)

    def project(c):
        cols = c.columns()
        part = lax.dot_general(da[...], wg[cols, :], LAST, preferred_element_type=F32)
        part += lax.dot_general(db[...], wu[cols, :], LAST, preferred_element_type=F32)
        c.buffers[half_send][c.k] = part[slots:2 * slots].astype(BF16)
        halves(c).start()
        c.buffers[own][c.k] = part[0:slots]

    def add_halves(c):
        halves(c).wait_recv()
        rows = (c.get(own) + c.get(half_recv).astype(F32)).astype(BF16)
        c.buffers[back_send][c.k] = rows.reshape(nodes, per_n, c.width)
        spread(4, c.sem, c.at(back_send), c.at(back_recv), False)

    def unsort(c):
        arrive(4, c.sem, c.at(back_recv), False)
        mid = c.width // 2
        rows = jnp.dot(
            list_lo[...], c.buffers[back_recv][c.k, :, :, 0:mid].reshape(slots, mid),
            preferred_element_type=F32,
        )
        rows += jnp.dot(
            list_hi[...], c.buffers[back_recv][c.k, :, :, mid:c.width].reshape(slots, mid),
            preferred_element_type=F32,
        )
        c.buffers[home_send][c.k] = rows.astype(BF16).reshape(zs, block, mid)
        spread(5, c.sem, c.at(home_send), c.at(home_recv), True)

    def gather(c):
        halves(c).wait_send()
        leave(4, c.sem, c.at(back_recv), nodes)
        arrive(5, c.sem, c.at(home_recv), True)
        rows = c.get(home_recv).reshape(listed, c.width // 2)
        for h, ref in enumerate((comb_lo, comb_hi)):
            out_ref[:, c.columns(h, 2)] = jnp.dot(
                ref[...], rows, preferred_element_type=F32
            ).astype(BF16)
        leave(5, c.sem, c.at(home_recv), zs)

    def when(i, lag, segments, stage):
        for segment, count in segments:
            start = segment[3] + lag

            @pl.when((i >= start) & (i < start + count))
            def _():
                stage(Chunk(segment, i - start))

    pl.semaphore_wait(barrier, zs + nodes - 1)
    spread(6, 0, meta_send, meta_recv, True, shared=True)
    early = [Chunk(segment, k) for segment, count in out_segments for k in range(count)][:AHEAD]
    for c in early:
        select(c)

    gates = jnp.where(by_first, gate_ref[0:1, :].astype(F32), gate_ref[1:2, :].astype(F32))
    weighted = chosen * expand(gates)
    turn = eye(toks)
    for ref, mask in ((comb_lo, ~upper), (comb_hi, upper)):
        ref[...] = lax.dot_general(
            turn, jnp.where(mask, weighted, 0.0).astype(BF16), LAST, preferred_element_type=F32
        ).astype(BF16)
    acc_a[...] = jnp.zeros_like(acc_a)
    acc_b[...] = jnp.zeros_like(acc_b)
    acc_d[...] = jnp.zeros_like(acc_d)

    arrive(6, 0, meta_recv, True)
    slot = iota((nodes * SLOTS, toks), 0)
    expert = slot // SLOTS * zs + z
    wanted = (slot % SLOTS).astype(F32)
    position = order[0:block]
    position = jnp.where(position >= cap, position - cap, position).astype(F32)
    wide = iota((nodes * SLOTS, slots), 1)
    narrow = iota((nodes * SLOTS, slots), 0)
    same = (wide // per_n == narrow // SLOTS) & (wide % SLOTS == narrow % SLOTS)
    lower = iota((block, slots), 0) < cap
    flags = meta_recv[0]
    for q in range(zs):
        if q:
            flags = jnp.maximum(flags, meta_recv[q])
        first = meta_recv[q, 0:1, 0:toks]
        second = meta_recv[q, 1:2, 0:toks]
        names = ((first == expert) | (second == expert)).astype(F32)
        names = jnp.where(before(names) == wanted, names, 0.0)
        on_list = (lax.rem(first, zs) == z) | (lax.rem(second, zs) == z)
        on_list = jnp.broadcast_to(on_list.astype(F32), (block, toks))
        on_list = jnp.where(before(on_list) == position, on_list, 0.0)
        table = lax.dot_general(
            on_list.astype(BF16), names.astype(BF16), LAST, preferred_element_type=F32
        )
        place_q = (same & ((wide % per_n) // SLOTS == q)).astype(F32).astype(BF16)
        table = jnp.dot(table.astype(BF16), place_q, preferred_element_type=F32)
        list_lo[q * block:(q + 1) * block, :] = jnp.where(lower, table, 0.0).astype(BF16)
        list_hi[q * block:(q + 1) * block, :] = jnp.where(lower, 0.0, table).astype(BF16)
    turn = eye(slots)
    sort_x[...] = lax.dot_general(turn, list_lo[...], LAST, preferred_element_type=F32).astype(BF16)
    sort_g[...] = lax.dot_general(turn, list_hi[...], LAST, preferred_element_type=F32).astype(BF16)
    flag_n_send[...] = flags
    spread(7, 0, flag_n_send, flag_n_recv, False, shared=True)

    def dispatch(i, carry):
        @pl.when(i + AHEAD < out_steps)
        def _():
            when(i, -AHEAD, out_segments, select)

        when(i, 0, out_segments, resort)

        @pl.when(i == 2)
        def _():
            for copy in weights:
                copy.wait()

        when(i, 2, out_segments, multiply)
        when(i, 1, out_segments, share)
        return carry

    lax.fori_loop(0, out_steps + 2, dispatch, 0)

    a = acc_a[...]
    sig = jax.nn.sigmoid(a)
    grad = acc_d[...] * sig
    da[...] = (grad * acc_b[...] * (1.0 + a * (1.0 - sig))).astype(BF16)
    db[...] = (grad * a).astype(BF16)

    other = remote(8, 0, flag_s_send, flag_s_recv, sibling)

    def combine_step(i, carry):
        when(i, 0, back_segments, project)
        when(i, 1, back_segments, add_halves)
        when(i, 2, back_segments, unsort)

        @pl.when(i == 4)
        def _():
            arrive(7, 0, flag_n_recv, False)
            flags = flag_n_recv[0]
            for m in range(1, nodes):
                flags = jnp.maximum(flags, flag_n_recv[m])
            flag_s_send[...] = flags
            other.start()

        when(i, 0, out_segments, release)
        when(i, 4, back_segments, gather)
        return carry

    lax.fori_loop(0, max(back_steps + 4, out_steps, 5), combine_step, 0)

    leave(6, 0, meta_recv, zs)
    leave(7, 0, flag_n_recv, nodes)
    other.wait()
    flag_ref[...] = jnp.maximum(flag_s_send[2:3, 0:1], flag_s_recv[2:3, 0:1])


def exchange(inputs, out_grad, experts, gates, gate_matrix, up_matrix, down_matrix):
    nodes = lax.axis_size("node")
    zs = lax.axis_size("local") // 2
    toks, model = inputs.shape
    hidden = gate_matrix.shape[2]
    per_n = zs * SLOTS
    slots = nodes * zs * SLOTS
    block = 2 * CAP
    listed = zs * block
    steps = max(sum(count for count, _ in segs) for segs in (OUT_SEGMENTS, BACK_SEGMENTS))
    vmem = pl.BlockSpec(memory_space=pltpu.VMEM)
    hbm = pl.BlockSpec(memory_space=pl.ANY)
    buffers = []
    for count, width in OUT_SEGMENTS:
        buffers += [
            pltpu.VMEM((count, zs, block, width), BF16),
            pltpu.VMEM((count, zs, block, width), BF16),
            pltpu.VMEM((count, nodes, 2 * per_n, width), BF16),
            pltpu.VMEM((count, 2, nodes, 2 * per_n, width), BF16),
        ]
    for count, width in BACK_SEGMENTS:
        buffers += [
            pltpu.VMEM((count, slots, width), F32),
            pltpu.VMEM((count, slots, width), BF16),
            pltpu.VMEM((count, slots, width), BF16),
            pltpu.VMEM((count, nodes, per_n, width), BF16),
            pltpu.VMEM((count, nodes, per_n, width), BF16),
            pltpu.VMEM((count, zs, block, width // 2), BF16),
            pltpu.VMEM((count, zs, block, width // 2), BF16),
        ]
    return pl.pallas_call(
        functools.partial(kernel, nodes, zs, CAP),
        out_shape=(
            jax.ShapeDtypeStruct((toks, model), BF16),
            jax.ShapeDtypeStruct((1, 1), jnp.int32),
        ),
        in_specs=[vmem] * 4 + [hbm] * 3,
        out_specs=(vmem, vmem),
        scratch_shapes=[
            pltpu.VMEM((listed, toks), BF16),
            pltpu.VMEM((listed, toks), BF16),
            pltpu.VMEM((toks, listed), BF16),
            pltpu.VMEM((toks, listed), BF16),
            pltpu.VMEM((slots, listed), BF16),
            pltpu.VMEM((slots, listed), BF16),
            pltpu.VMEM((listed, slots), BF16),
            pltpu.VMEM((listed, slots), BF16),
            pltpu.VMEM((model, hidden), BF16),
            pltpu.VMEM((model, hidden), BF16),
            pltpu.VMEM((hidden, model), BF16),
            pltpu.VMEM((2 * slots, hidden), F32),
            pltpu.VMEM((2 * slots, hidden), F32),
            pltpu.VMEM((2 * slots, hidden), F32),
            pltpu.VMEM((2 * slots, hidden), BF16),
            pltpu.VMEM((2 * slots, hidden), BF16),
            pltpu.VMEM((8, 128), jnp.int32),
            pltpu.VMEM((zs, 8, 128), jnp.int32),
            pltpu.VMEM((8, 128), jnp.int32),
            pltpu.VMEM((nodes, 8, 128), jnp.int32),
            pltpu.VMEM((8, 128), jnp.int32),
            pltpu.VMEM((8, 128), jnp.int32),
            pltpu.SemaphoreType.DMA((3,)),
            pltpu.SemaphoreType.DMA((9, steps)),
            pltpu.SemaphoreType.DMA((9, steps)),
            pltpu.SemaphoreType.DMA((9, steps)),
        ] + buffers,
        compiler_params=pltpu.CompilerParams(
            collective_id=0, has_side_effects=True, vmem_limit_bytes=60 * 1024 * 1024
        ),
        name="experts_backward",
    )(inputs, out_grad, experts, gates, gate_matrix, up_matrix, down_matrix)


def expert_rows(x_slots, grad_slots, gate_slots, gate_matrix, up_matrix, down_matrix):
    layout = x_slots.shape
    model_width = layout[-1]
    x_rows = x_slots.reshape(-1, model_width)
    grad_rows = grad_slots.reshape(-1, model_width)
    gate_rows = gate_slots.reshape(-1).astype(jnp.float32)
    w_gate = gate_matrix[0]
    w_up = up_matrix[0]
    w_down = down_matrix[0]
    contract_last = (((1,), (1,)), ((), ()))
    pre_gate = jnp.dot(x_rows, w_gate, preferred_element_type=jnp.float32)
    pre_up = jnp.dot(x_rows, w_up, preferred_element_type=jnp.float32)
    hidden_grad = gate_rows[:, None] * lax.dot_general(
        grad_rows, w_down, contract_last, preferred_element_type=jnp.float32
    )
    sig = jax.nn.sigmoid(pre_gate)
    grad_gate = (hidden_grad * pre_up * sig * (1.0 + pre_gate * (1.0 - sig))).astype(jnp.bfloat16)
    grad_up = (hidden_grad * pre_gate * sig).astype(jnp.bfloat16)
    result = lax.dot_general(grad_gate, w_gate, contract_last, preferred_element_type=jnp.float32)
    result = result + lax.dot_general(
        grad_up, w_up, contract_last, preferred_element_type=jnp.float32
    )
    return result.astype(jnp.bfloat16).reshape(layout)


def padded(inputs, out_grad, experts, gate_values, gate_matrix, up_matrix, down_matrix):
    node_count = lax.axis_size("node")
    local_count = lax.axis_size("local")
    per_node = local_count // 2
    tok_count, model_width = inputs.shape
    expert_count = node_count * per_node
    node_cap = min(tok_count, 2 * tok_count * 1 // node_count)
    slot_cap = 2 * node_cap // per_node
    expert_hits = experts[:, :, None] == jnp.arange(expert_count, dtype=jnp.int32)
    routed = jnp.any(expert_hits, axis=1).astype(jnp.int32)
    gate_table = jnp.sum(
        jnp.where(expert_hits, gate_values[:, :, None], jnp.zeros((), jnp.bfloat16)), axis=1
    )
    slot_rank = jnp.cumsum(routed, axis=0) - routed
    slot_pick = (routed[:, :, None] == 1) & (
        slot_rank[:, :, None] == jnp.arange(slot_cap, dtype=jnp.int32)
    )
    slot_select = jnp.transpose(slot_pick.astype(jnp.bfloat16), (1, 2, 0))
    gate_slot = jnp.sum(
        jnp.where(slot_pick, gate_table[:, :, None], jnp.zeros((), jnp.bfloat16)), axis=0
    )
    x_slots = jnp.einsum(
        "ect,td->ecd", slot_select, inputs, preferred_element_type=jnp.float32
    ).astype(jnp.bfloat16)
    grad_slots = jnp.einsum(
        "ect,td->ecd", slot_select, out_grad, preferred_element_type=jnp.float32
    ).astype(jnp.bfloat16)
    x_slots = jnp.repeat(x_slots.reshape(node_count, per_node, slot_cap, model_width), 2, axis=1)
    grad_slots = jnp.repeat(
        grad_slots.reshape(node_count, per_node, slot_cap, model_width), 2, axis=1
    )
    gate_slot = jnp.repeat(gate_slot.reshape(node_count, per_node, slot_cap), 2, axis=1)
    x_slots, grad_slots, gate_slot = (
        lax.all_to_all(x_slots, "node", split_axis=0, concat_axis=0, tiled=True),
        lax.all_to_all(grad_slots, "node", split_axis=0, concat_axis=0, tiled=True),
        lax.all_to_all(gate_slot, "node", split_axis=0, concat_axis=0, tiled=True),
    )
    x_slots, grad_slots, gate_slot = (
        lax.all_to_all(x_slots, "local", split_axis=1, concat_axis=1, tiled=True),
        lax.all_to_all(grad_slots, "local", split_axis=1, concat_axis=1, tiled=True),
        lax.all_to_all(gate_slot, "local", split_axis=1, concat_axis=1, tiled=True),
    )
    partials = expert_rows(x_slots, grad_slots, gate_slot, gate_matrix, up_matrix, down_matrix)
    returned = lax.all_to_all(partials, "local", split_axis=1, concat_axis=1, tiled=True)
    returned = lax.all_to_all(returned, "node", split_axis=0, concat_axis=0, tiled=True)
    select_half = jnp.repeat(
        slot_select.reshape(node_count, per_node, slot_cap, tok_count), 2, axis=1
    )
    node_sums = jnp.einsum(
        "mlct,mlcd->mtd", select_half, returned, preferred_element_type=jnp.float32
    ).astype(jnp.bfloat16)
    total = jnp.sum(node_sums.astype(jnp.float32), axis=0)
    return total.astype(jnp.bfloat16)


def shards(inputs, out_grad, experts, gate_values, gate_matrix, up_matrix, down_matrix):
    weights = (gate_matrix, up_matrix, down_matrix)
    result, flag = exchange(inputs, out_grad, experts.T, gate_values.T, *weights)
    return lax.cond(
        flag[0, 0] > 0,
        lambda: padded(inputs, out_grad, experts, gate_values, *weights),
        lambda: result,
    )


def solution(mesh):
    rows = P(("node", "local"), None)
    stack = P(("node", "local"), None, None)
    return jax.shard_map(
        shards, mesh=mesh, in_specs=(rows,) * 4 + (stack,) * 3, out_specs=rows, check_vma=False
    )
```

```python
import functools
import math

import jax
import jax.numpy as jnp
from jax import lax
from jax.experimental import pallas as pl
from jax.experimental.pallas import tpu as pltpu
from jax.sharding import PartitionSpec as P

SLOTS = 2
CAP = 24
OUT_SEGMENTS = ((14, 256),)
BACK_SEGMENTS = ((7, 512),)
AHEAD = 4
GROUP = 1
GATHER_LAG = 4
MESH = pl.DeviceIdType.MESH
LAST = (((1,), (1,)), ((), ()))
F32 = jnp.float32
BF16 = jnp.bfloat16


def iota(shape, dim):
    return lax.broadcasted_iota(jnp.int32, shape, dim)


def eye(n):
    return (iota((n, n), 0) == iota((n, n), 1)).astype(BF16)


class Chunk:
    def __init__(self, segment, k):
        self.buffers, self.width, self.begin, self.first = segment
        self.k = k
        self.sem = self.first + k

    def columns(self, part=0, parts=1):
        size = self.width // parts
        start = self.begin + self.k * self.width + part * size
        return pl.ds(start if isinstance(start, int) else pl.multiple_of(start, 128), size)

    def at(self, i, *rest):
        return self.buffers[i].at[(self.k, *rest)]

    def get(self, i):
        return self.buffers[i][self.k]


def split(segments, refs):
    result, begin, first = [], 0, 0
    each = len(refs) // len(segments)
    for n, (count, width) in enumerate(segments):
        result.append(((refs[n * each:(n + 1) * each], width, begin, first), count))
        begin += count * width
        first += count
    return result, first


def kernel(
    nodes, zs, cap,
    x_hbm, g_hbm, exp_ref, gate_ref, wg_hbm, wu_hbm, wd_hbm, out_hbm, flag_ref,
    x_ref, g_ref, out_ref,
    pick_x, pick_g, comb_lo, comb_hi, sort_x, sort_g, list_lo, list_hi,
    wg, wu, wd, acc_a, acc_b, acc_d, da, db,
    meta_send, meta_recv, flag_n_send, flag_n_recv, flag_s_send, flag_s_recv,
    w_sem, send_sem, recv_sem, local_sem, out_sem, *rest,
):
    z_send, z_recv, n_send, n_recv = range(4)
    own, half_send, half_recv, back_send, back_recv, home_send, home_recv = range(7)
    out_segments, out_steps = split(OUT_SEGMENTS, rest[:4 * len(OUT_SEGMENTS)])
    back_segments, back_steps = split(BACK_SEGMENTS, rest[4 * len(OUT_SEGMENTS):])
    node = lax.axis_index("node")
    local = lax.axis_index("local")
    z = local // 2
    core = local % 2
    sibling = (node, z * 2 + (1 - core))
    toks = x_hbm.shape[0]
    per_n = zs * SLOTS
    slots = nodes * zs * SLOTS
    block = 2 * cap
    listed = zs * block

    side = math.isqrt(nodes)
    z_steps = sorted(range(1, zs), key=lambda j: (-min(j, zs - j), j))
    node_steps = sorted(
        ((a, b) for a in range(side) for b in range(side) if a or b),
        key=lambda s: (-min(s[0], side - s[0]) - min(s[1], side - s[1]), s),
    )

    tokens = [
        pltpu.make_async_copy(src, dst, w_sem.at[3 + i])
        for i, (src, dst) in enumerate(((x_hbm, x_ref), (g_hbm, g_ref)))
    ]
    for copy in tokens:
        copy.start()
    weights = [
        pltpu.make_async_copy(src.at[0], dst, w_sem.at[i])
        for i, (src, dst) in enumerate(((wg_hbm, wg), (wu_hbm, wu), (wd_hbm, wd)))
    ]
    for copy in weights:
        copy.start()

    barrier = pltpu.get_barrier_semaphore()
    for j in range(1, zs):
        pl.semaphore_signal(
            barrier, inc=1, device_id=(node, lax.rem(z + j, zs) * 2 + core), device_id_type=MESH
        )
    for j in range(1, nodes):
        pl.semaphore_signal(
            barrier, inc=1, device_id=(lax.rem(node + j, nodes), local), device_id_type=MESH
        )
    pl.semaphore_signal(barrier, inc=1, device_id=sibling, device_id_type=MESH)

    earlier = (iota((toks, toks), 0) < iota((toks, toks), 1)).astype(BF16)

    def before(mask):
        return jnp.dot(mask.astype(BF16), earlier, preferred_element_type=F32)

    first = exp_ref[0:1, :]
    second = exp_ref[1:2, :]
    target = iota((zs, toks), 0)
    by_first = lax.rem(first, zs) == target
    by_second = lax.rem(second, zs) == target
    on_list = (by_first | by_second).astype(F32)

    def expand(rows):
        return jnp.broadcast_to(rows[:, None, :], (zs, block, toks)).reshape(listed, toks)

    order = iota((zs, block, toks), 1).reshape(listed, toks)
    upper = order >= cap
    place = jnp.where(upper, order - cap, order).astype(F32)
    chosen = jnp.where(expand(before(on_list)) == place, expand(on_list), 0.0)
    pick_x[...] = jnp.where(upper, 0.0, chosen).astype(BF16)
    pick_g[...] = jnp.where(upper, chosen, 0.0).astype(BF16)
    longest = jnp.max(jnp.sum(on_list, axis=1, keepdims=True), axis=0, keepdims=True)
    over = (longest > cap).astype(F32).astype(jnp.int32)
    meta_send[...] = jnp.zeros_like(meta_send) + over
    meta_send[0:1, 0:toks] = first
    meta_send[1:2, 0:toks] = second

    def remote(phase, k, src, dst, device):
        return pltpu.make_async_remote_copy(
            src_ref=src, dst_ref=dst, send_sem=send_sem.at[phase, k],
            recv_sem=recv_sem.at[phase, k], device_id=device, device_id_type=MESH,
        )

    def spread(phase, k, src, dst, along_z, shared=False):
        here, count = (z, zs) if along_z else (node, nodes)
        mine = src if shared else src.at[here]
        pltpu.make_async_copy(mine, dst.at[here], local_sem.at[phase, k]).start()
        for step in z_steps if along_z else node_steps:
            if along_z:
                to = lax.rem(z + step, zs)
                device = (node, to * 2 + core)
            else:
                to = lax.rem(node // side + step[0], side) * side + lax.rem(node % side + step[1], side)
                device = (to, local)
            remote(phase, k, src if shared else src.at[to], dst.at[here], device).start()

    def arrive(phase, k, dst, along_z):
        here, count = (z, zs) if along_z else (node, nodes)
        pltpu.make_async_copy(dst.at[here], dst.at[here], local_sem.at[phase, k]).wait()
        rest = pl.ds(0, count - 1)
        remote(phase, k, dst.at[rest], dst.at[rest], sibling).wait_recv()

    def leave(phase, k, dst, count):
        rest = pl.ds(0, count - 1)
        remote(phase, k, dst.at[rest], dst.at[rest], sibling).wait_send()

    def select(c):
        rows = jnp.dot(pick_x[...], x_ref[:, c.columns()], preferred_element_type=F32)
        rows += jnp.dot(pick_g[...], g_ref[:, c.columns()], preferred_element_type=F32)
        c.buffers[z_send][c.k] = rows.astype(BF16).reshape(zs, block, c.width)
        spread(0, c.sem, c.at(z_send), c.at(z_recv), True)

    def resort(c):
        arrive(0, c.sem, c.at(z_recv), True)
        rows = c.get(z_recv).reshape(listed, c.width)
        for h, ref in enumerate((sort_x, sort_g)):
            part = jnp.dot(ref[...], rows, preferred_element_type=F32)
            c.buffers[n_send][c.k, :, h * per_n:(h + 1) * per_n, :] = part.astype(BF16).reshape(
                nodes, per_n, c.width
            )
        spread(1, c.sem, c.at(n_send), c.at(n_recv, 0), False)

    def to_sibling(c):
        return remote(2, c.sem, c.at(n_recv, 0), c.at(n_recv, 1), sibling)

    def share(c):
        arrive(1, c.sem, c.at(n_recv, 0), False)
        to_sibling(c).start()

    def multiply(segment, k):
        group = [Chunk(segment, k + n) for n in range(GROUP)]
        for c in group:
            to_sibling(c).wait_recv()
        width = segment[1]
        start = segment[2] + k * width
        cols = pl.ds(pl.multiple_of(start, 128), GROUP * width)

        def joined(part):
            return jnp.concatenate(
                [
                    c.buffers[n_recv][c.k, :, :, part * per_n:(part + 1) * per_n, :].reshape(
                        2 * slots, width
                    )
                    for c in group
                ],
                axis=1,
            )

        rows = joined(0)
        acc_a[...] += jnp.dot(rows, wg[cols, :], preferred_element_type=F32)
        acc_b[...] += jnp.dot(rows, wu[cols, :], preferred_element_type=F32)
        acc_d[...] += lax.dot_general(joined(1), wd[:, cols], LAST, preferred_element_type=F32)

    def release(c):
        leave(0, c.sem, c.at(z_recv), zs)
        leave(1, c.sem, c.at(n_recv, 0), nodes)
        to_sibling(c).wait_send()

    def halves(c):
        return remote(3, c.sem, c.at(half_send), c.at(half_recv), sibling)

    def project(c):
        cols = c.columns()
        part = lax.dot_general(da[...], wg[cols, :], LAST, preferred_element_type=F32)
        part += lax.dot_general(db[...], wu[cols, :], LAST, preferred_element_type=F32)
        c.buffers[half_send][c.k] = part[slots:2 * slots].astype(BF16)
        halves(c).start()
        c.buffers[own][c.k] = part[0:slots]

    def add_halves(c):
        halves(c).wait_recv()
        rows = (c.get(own) + c.get(half_recv).astype(F32)).astype(BF16)
        c.buffers[back_send][c.k] = rows.reshape(nodes, per_n, c.width)
        spread(4, c.sem, c.at(back_send), c.at(back_recv), False)

    def unsort(c):
        arrive(4, c.sem, c.at(back_recv), False)
        mid = c.width // 2
        rows = jnp.dot(
            list_lo[...], c.buffers[back_recv][c.k, :, :, 0:mid].reshape(slots, mid),
            preferred_element_type=F32,
        )
        rows += jnp.dot(
            list_hi[...], c.buffers[back_recv][c.k, :, :, mid:c.width].reshape(slots, mid),
            preferred_element_type=F32,
        )
        c.buffers[home_send][c.k] = rows.astype(BF16).reshape(zs, block, mid)
        spread(5, c.sem, c.at(home_send), c.at(home_recv), True)

    def gather(c):
        halves(c).wait_send()
        leave(4, c.sem, c.at(back_recv), nodes)
        arrive(5, c.sem, c.at(home_recv), True)
        rows = c.get(home_recv).reshape(listed, c.width // 2)
        for h, ref in enumerate((comb_lo, comb_hi)):
            out_ref[:, c.columns(h, 2)] = jnp.dot(
                ref[...], rows, preferred_element_type=F32
            ).astype(BF16)
        result(c).start()
        leave(5, c.sem, c.at(home_recv), zs)

    def result(c):
        cols = c.columns()
        return pltpu.make_async_copy(
            out_ref.at[:, cols], out_hbm.at[:, cols], out_sem.at[c.sem]
        )

    def when(i, lag, segments, stage):
        for segment, count in segments:
            start = segment[3] + lag

            @pl.when((i >= start) & (i < start + count))
            def _():
                stage(Chunk(segment, i - start))

    pl.semaphore_wait(barrier, zs + nodes - 1)
    spread(6, 0, meta_send, meta_recv, True, shared=True)
    for copy in tokens:
        copy.wait()
    early = [Chunk(segment, k) for segment, count in out_segments for k in range(count)][:AHEAD]
    for c in early:
        select(c)

    gates = jnp.where(by_first, gate_ref[0:1, :].astype(F32), gate_ref[1:2, :].astype(F32))
    weighted = chosen * expand(gates)
    turn = eye(toks)
    for ref, mask in ((comb_lo, ~upper), (comb_hi, upper)):
        ref[...] = lax.dot_general(
            turn, jnp.where(mask, weighted, 0.0).astype(BF16), LAST, preferred_element_type=F32
        ).astype(BF16)
    acc_a[...] = jnp.zeros_like(acc_a)
    acc_b[...] = jnp.zeros_like(acc_b)
    acc_d[...] = jnp.zeros_like(acc_d)

    arrive(6, 0, meta_recv, True)
    slot = iota((nodes * SLOTS, toks), 0)
    expert = slot // SLOTS * zs + z
    wanted = (slot % SLOTS).astype(F32)
    position = order[0:block]
    position = jnp.where(position >= cap, position - cap, position).astype(F32)
    wide = iota((nodes * SLOTS, slots), 1)
    narrow = iota((nodes * SLOTS, slots), 0)
    same = (wide // per_n == narrow // SLOTS) & (wide % SLOTS == narrow % SLOTS)
    lower = iota((block, slots), 0) < cap
    flags = meta_recv[0]
    for q in range(zs):
        if q:
            flags = jnp.maximum(flags, meta_recv[q])
        first = meta_recv[q, 0:1, 0:toks]
        second = meta_recv[q, 1:2, 0:toks]
        names = ((first == expert) | (second == expert)).astype(F32)
        names = jnp.where(before(names) == wanted, names, 0.0)
        on_list = (lax.rem(first, zs) == z) | (lax.rem(second, zs) == z)
        on_list = jnp.broadcast_to(on_list.astype(F32), (block, toks))
        on_list = jnp.where(before(on_list) == position, on_list, 0.0)
        table = lax.dot_general(
            on_list.astype(BF16), names.astype(BF16), LAST, preferred_element_type=F32
        )
        place_q = (same & ((wide % per_n) // SLOTS == q)).astype(F32).astype(BF16)
        table = jnp.dot(table.astype(BF16), place_q, preferred_element_type=F32)
        list_lo[q * block:(q + 1) * block, :] = jnp.where(lower, table, 0.0).astype(BF16)
        list_hi[q * block:(q + 1) * block, :] = jnp.where(lower, 0.0, table).astype(BF16)
    turn = eye(slots)
    sort_x[...] = lax.dot_general(turn, list_lo[...], LAST, preferred_element_type=F32).astype(BF16)
    sort_g[...] = lax.dot_general(turn, list_hi[...], LAST, preferred_element_type=F32).astype(BF16)
    flag_n_send[...] = flags
    spread(7, 0, flag_n_send, flag_n_recv, False, shared=True)

    def dispatch(i, carry):
        @pl.when(i + AHEAD < out_steps)
        def _():
            when(i, -AHEAD, out_segments, select)

        when(i, 0, out_segments, resort)

        @pl.when(i == 2)
        def _():
            for copy in weights:
                copy.wait()

        for segment, count in out_segments:
            start = segment[3] + GROUP + 1

            @pl.when((i >= start) & (i < start + count) & ((i - start) % GROUP == 0))
            def _():
                multiply(segment, i - start)

        when(i, 1, out_segments, share)
        return carry

    lax.fori_loop(0, out_steps + 2, dispatch, 0)

    a = acc_a[...]
    sig = jax.nn.sigmoid(a)
    grad = acc_d[...] * sig
    da[...] = (grad * acc_b[...] * (1.0 + a * (1.0 - sig))).astype(BF16)
    db[...] = (grad * a).astype(BF16)

    other = remote(8, 0, flag_s_send, flag_s_recv, sibling)

    def combine_step(i, carry):
        when(i, 0, back_segments, project)
        when(i, 1, back_segments, add_halves)
        when(i, 2, back_segments, unsort)

        @pl.when(i == 4)
        def _():
            arrive(7, 0, flag_n_recv, False)
            flags = flag_n_recv[0]
            for m in range(1, nodes):
                flags = jnp.maximum(flags, flag_n_recv[m])
            flag_s_send[...] = flags
            other.start()

        when(i, 0, out_segments, release)
        when(i, GATHER_LAG, back_segments, gather)
        when(i, GATHER_LAG + 1, back_segments, lambda c: result(c).wait())
        return carry

    lax.fori_loop(0, max(back_steps + GATHER_LAG + 1, out_steps, 5), combine_step, 0)

    leave(6, 0, meta_recv, zs)
    leave(7, 0, flag_n_recv, nodes)
    other.wait()
    flag_ref[...] = jnp.maximum(flag_s_send[2:3, 0:1], flag_s_recv[2:3, 0:1])


def exchange(inputs, out_grad, experts, gates, gate_matrix, up_matrix, down_matrix):
    nodes = lax.axis_size("node")
    zs = lax.axis_size("local") // 2
    toks, model = inputs.shape
    hidden = gate_matrix.shape[2]
    per_n = zs * SLOTS
    slots = nodes * zs * SLOTS
    block = 2 * CAP
    listed = zs * block
    steps = max(sum(count for count, _ in segs) for segs in (OUT_SEGMENTS, BACK_SEGMENTS))
    vmem = pl.BlockSpec(memory_space=pltpu.VMEM)
    hbm = pl.BlockSpec(memory_space=pl.ANY)
    buffers = []
    for count, width in OUT_SEGMENTS:
        buffers += [
            pltpu.VMEM((count, zs, block, width), BF16),
            pltpu.VMEM((count, zs, block, width), BF16),
            pltpu.VMEM((count, nodes, 2 * per_n, width), BF16),
            pltpu.VMEM((count, 2, nodes, 2 * per_n, width), BF16),
        ]
    for count, width in BACK_SEGMENTS:
        buffers += [
            pltpu.VMEM((count, slots, width), F32),
            pltpu.VMEM((count, slots, width), BF16),
            pltpu.VMEM((count, slots, width), BF16),
            pltpu.VMEM((count, nodes, per_n, width), BF16),
            pltpu.VMEM((count, nodes, per_n, width), BF16),
            pltpu.VMEM((count, zs, block, width // 2), BF16),
            pltpu.VMEM((count, zs, block, width // 2), BF16),
        ]
    return pl.pallas_call(
        functools.partial(kernel, nodes, zs, CAP),
        out_shape=(
            jax.ShapeDtypeStruct((toks, model), BF16),
            jax.ShapeDtypeStruct((1, 1), jnp.int32),
        ),
        in_specs=[hbm] * 2 + [vmem] * 2 + [hbm] * 3,
        out_specs=(hbm, vmem),
        scratch_shapes=[
            pltpu.VMEM((toks, model), BF16),
            pltpu.VMEM((toks, model), BF16),
            pltpu.VMEM((toks, model), BF16),
            pltpu.VMEM((listed, toks), BF16),
            pltpu.VMEM((listed, toks), BF16),
            pltpu.VMEM((toks, listed), BF16),
            pltpu.VMEM((toks, listed), BF16),
            pltpu.VMEM((slots, listed), BF16),
            pltpu.VMEM((slots, listed), BF16),
            pltpu.VMEM((listed, slots), BF16),
            pltpu.VMEM((listed, slots), BF16),
            pltpu.VMEM((model, hidden), BF16),
            pltpu.VMEM((model, hidden), BF16),
            pltpu.VMEM((hidden, model), BF16),
            pltpu.VMEM((2 * slots, hidden), F32),
            pltpu.VMEM((2 * slots, hidden), F32),
            pltpu.VMEM((2 * slots, hidden), F32),
            pltpu.VMEM((2 * slots, hidden), BF16),
            pltpu.VMEM((2 * slots, hidden), BF16),
            pltpu.VMEM((8, 128), jnp.int32),
            pltpu.VMEM((zs, 8, 128), jnp.int32),
            pltpu.VMEM((8, 128), jnp.int32),
            pltpu.VMEM((nodes, 8, 128), jnp.int32),
            pltpu.VMEM((8, 128), jnp.int32),
            pltpu.VMEM((8, 128), jnp.int32),
            pltpu.SemaphoreType.DMA((5,)),
            pltpu.SemaphoreType.DMA((9, steps)),
            pltpu.SemaphoreType.DMA((9, steps)),
            pltpu.SemaphoreType.DMA((9, steps)),
            pltpu.SemaphoreType.DMA((steps,)),
        ] + buffers,
        compiler_params=pltpu.CompilerParams(
            collective_id=0, has_side_effects=True, vmem_limit_bytes=60 * 1024 * 1024
        ),
        name="experts_backward",
    )(inputs, out_grad, experts, gates, gate_matrix, up_matrix, down_matrix)


def expert_rows(x_slots, grad_slots, gate_slots, gate_matrix, up_matrix, down_matrix):
    layout = x_slots.shape
    model_width = layout[-1]
    x_rows = x_slots.reshape(-1, model_width)
    grad_rows = grad_slots.reshape(-1, model_width)
    gate_rows = gate_slots.reshape(-1).astype(jnp.float32)
    w_gate = gate_matrix[0]
    w_up = up_matrix[0]
    w_down = down_matrix[0]
    contract_last = (((1,), (1,)), ((), ()))
    pre_gate = jnp.dot(x_rows, w_gate, preferred_element_type=jnp.float32)
    pre_up = jnp.dot(x_rows, w_up, preferred_element_type=jnp.float32)
    hidden_grad = gate_rows[:, None] * lax.dot_general(
        grad_rows, w_down, contract_last, preferred_element_type=jnp.float32
    )
    sig = jax.nn.sigmoid(pre_gate)
    grad_gate = (hidden_grad * pre_up * sig * (1.0 + pre_gate * (1.0 - sig))).astype(jnp.bfloat16)
    grad_up = (hidden_grad * pre_gate * sig).astype(jnp.bfloat16)
    result = lax.dot_general(grad_gate, w_gate, contract_last, preferred_element_type=jnp.float32)
    result = result + lax.dot_general(
        grad_up, w_up, contract_last, preferred_element_type=jnp.float32
    )
    return result.astype(jnp.bfloat16).reshape(layout)


def padded(inputs, out_grad, experts, gate_values, gate_matrix, up_matrix, down_matrix):
    node_count = lax.axis_size("node")
    local_count = lax.axis_size("local")
    per_node = local_count // 2
    tok_count, model_width = inputs.shape
    expert_count = node_count * per_node
    node_cap = min(tok_count, 2 * tok_count * 1 // node_count)
    slot_cap = 2 * node_cap // per_node
    expert_hits = experts[:, :, None] == jnp.arange(expert_count, dtype=jnp.int32)
    routed = jnp.any(expert_hits, axis=1).astype(jnp.int32)
    gate_table = jnp.sum(
        jnp.where(expert_hits, gate_values[:, :, None], jnp.zeros((), jnp.bfloat16)), axis=1
    )
    slot_rank = jnp.cumsum(routed, axis=0) - routed
    slot_pick = (routed[:, :, None] == 1) & (
        slot_rank[:, :, None] == jnp.arange(slot_cap, dtype=jnp.int32)
    )
    slot_select = jnp.transpose(slot_pick.astype(jnp.bfloat16), (1, 2, 0))
    gate_slot = jnp.sum(
        jnp.where(slot_pick, gate_table[:, :, None], jnp.zeros((), jnp.bfloat16)), axis=0
    )
    x_slots = jnp.einsum(
        "ect,td->ecd", slot_select, inputs, preferred_element_type=jnp.float32
    ).astype(jnp.bfloat16)
    grad_slots = jnp.einsum(
        "ect,td->ecd", slot_select, out_grad, preferred_element_type=jnp.float32
    ).astype(jnp.bfloat16)
    x_slots = jnp.repeat(x_slots.reshape(node_count, per_node, slot_cap, model_width), 2, axis=1)
    grad_slots = jnp.repeat(
        grad_slots.reshape(node_count, per_node, slot_cap, model_width), 2, axis=1
    )
    gate_slot = jnp.repeat(gate_slot.reshape(node_count, per_node, slot_cap), 2, axis=1)
    x_slots, grad_slots, gate_slot = (
        lax.all_to_all(x_slots, "node", split_axis=0, concat_axis=0, tiled=True),
        lax.all_to_all(grad_slots, "node", split_axis=0, concat_axis=0, tiled=True),
        lax.all_to_all(gate_slot, "node", split_axis=0, concat_axis=0, tiled=True),
    )
    x_slots, grad_slots, gate_slot = (
        lax.all_to_all(x_slots, "local", split_axis=1, concat_axis=1, tiled=True),
        lax.all_to_all(grad_slots, "local", split_axis=1, concat_axis=1, tiled=True),
        lax.all_to_all(gate_slot, "local", split_axis=1, concat_axis=1, tiled=True),
    )
    partials = expert_rows(x_slots, grad_slots, gate_slot, gate_matrix, up_matrix, down_matrix)
    returned = lax.all_to_all(partials, "local", split_axis=1, concat_axis=1, tiled=True)
    returned = lax.all_to_all(returned, "node", split_axis=0, concat_axis=0, tiled=True)
    select_half = jnp.repeat(
        slot_select.reshape(node_count, per_node, slot_cap, tok_count), 2, axis=1
    )
    node_sums = jnp.einsum(
        "mlct,mlcd->mtd", select_half, returned, preferred_element_type=jnp.float32
    ).astype(jnp.bfloat16)
    total = jnp.sum(node_sums.astype(jnp.float32), axis=0)
    return total.astype(jnp.bfloat16)


def shards(inputs, out_grad, experts, gate_values, gate_matrix, up_matrix, down_matrix):
    weights = (gate_matrix, up_matrix, down_matrix)
    result, flag = exchange(inputs, out_grad, experts.T, gate_values.T, *weights)
    return lax.cond(
        flag[0, 0] > 0,
        lambda: padded(inputs, out_grad, experts, gate_values, *weights),
        lambda: result,
    )


def solution(mesh):
    rows = P(("node", "local"), None)
    stack = P(("node", "local"), None, None)
    return jax.shard_map(
        shards, mesh=mesh, in_specs=(rows,) * 4 + (stack,) * 3, out_specs=rows, check_vma=False
    )
```
